32 devices in a mesh: row: 4 (over x, core), col: 8 (over z, y).
Axes of the slice: x: 2, y: 2, z: 4, core: 2. Of those that a mesh axis runs over, the one named last changes fastest.
Arguments:
- object_tiles: float32 [2, 2, 512, 1024], P(None, None, 'row', 'col'), may hold values from -3 to 3
- positions: int32 [4, 8, 6, 2], P('row', 'col'), may hold values from 0 to 128, as said below
- probe: float32 [2, 128, 128], replicated, may hold values from -4.2 to 4.2
- phase: float32 [128, 128], replicated, may hold values from -3.140625 to 3.140625
- intensity: float32 [4, 8, 6, 128, 128], P('row', 'col'), may hold values from 0.05 to 1
Outputs:
- updated_tiles: float32 [2, 2, 1024, 2048], P(None, None, 'row', 'col')
The draws below stay inside these ranges and needn't reach their ends.
Inputs may be any that keep to these rules, and one draw needn't show every extreme that they name: `positions`: every window of 128 x 128 pixels lies inside the object. In every tile probe 0 takes the least and probe 1 the greatest row offset that this allows, probe 2 the least and probe 3 the greatest column offset.
All inputs are finite; a program needn't handle non-finite values.
Results may differ from the reference program's by a relative error of at most 0.0003.
Values sent between devices are 32-bit elements; how exact they have to be, the bound alone decides.
A program may use at most 64 MiB of HBM per device.

```python
import math
import jax
import jax.numpy as jnp
from jax import lax

PROBE = 128
PROBES = 6
MARGIN = 64
TILE = 128
PADW = 256
TROWS = 4
TCOLS = 8


def draw_positions(key, part):
    reach_max = PADW - PROBE
    tile_row = jnp.arange(TROWS, dtype=jnp.int32)[:, None, None]
    tile_col = jnp.arange(TCOLS, dtype=jnp.int32)[None, :, None]
    number = jnp.arange(PROBES, dtype=jnp.int32)[None, None, :]
    low_row = jnp.where(tile_row == 0, MARGIN, 0)
    high_row = jnp.where(tile_row == TROWS - 1, reach_max - MARGIN, reach_max)
    low_col = jnp.where(tile_col == 0, MARGIN, 0)
    high_col = jnp.where(tile_col == TCOLS - 1, reach_max - MARGIN, reach_max)
    raw_bits = jax.random.randint(key, (TROWS, TCOLS, PROBES, 2), 0, 1 << 20, dtype=jnp.int32)
    row_offsets = low_row + raw_bits[..., 0] % (high_row - low_row + 1)
    row_offsets = jnp.where(number == 0, low_row, jnp.where(number == 1, high_row, row_offsets))
    col_offsets = low_col + raw_bits[..., 1] % (high_col - low_col + 1)
    col_offsets = jnp.where(number == 2, low_col, jnp.where(number == 3, high_col, col_offsets))
    return jnp.stack([row_offsets, col_offsets], -1).astype(jnp.int32)


def shard_levels(own_key, extent, split, low, largest):
    factor_of, own = 1.0, jax.random.fold_in(own_key, 6)
    for position, blocks in split:
        heights = jnp.exp(jax.random.uniform(jax.random.fold_in(own, position), (blocks,), jnp.float32, low / len(split), largest / len(split)))
        factor_of = factor_of * jnp.repeat(heights, extent[position] // blocks).reshape([-1 if axis == position else 1 for axis in range(len(extent))])
    return factor_of


def bell_draw(stream_key, dims, spread, bound, split=(), kind=jnp.bfloat16):
    entries = spread * jax.random.normal(stream_key, dims, jnp.float32)
    if split:
        entries = entries * shard_levels(stream_key, dims, split, -0.22, 0.18)
    return jnp.clip(entries, -bound, bound).astype(kind)


def setup_inputs(seed: int = 0) -> dict:
    keys = jax.random.split(jax.random.key(seed), 6)
    object_tiles = bell_draw(keys[0], (2, 2, TROWS * TILE, TCOLS * TILE), 0.5, 3.0, ((2, 4), (3, 8)), jnp.float32)
    positions = draw_positions(jax.random.fold_in(keys[5], 71), 0)
    probe = bell_draw(keys[2], (2, PROBE, PROBE), 0.7, 4.2, (), jnp.float32)
    phase = jnp.clip(jax.random.uniform(keys[3], (PROBE, PROBE), jnp.float32, -3.140625, 3.140625), -3.140625, 3.140625)
    intensity = jnp.clip(jnp.exp(math.log(1.0) - 2.9957323 * jax.random.uniform(keys[4], (TROWS, TCOLS, PROBES, PROBE, PROBE), jnp.float32) ** shard_levels(keys[4], (TROWS, TCOLS, PROBES, PROBE, PROBE), ((0, 4), (1, 8)), -0.2, 0.2)), 0.05, 1.0)
    return {"object_tiles": object_tiles, "positions": positions, "probe": probe, "phase": phase, "intensity": intensity}


step_size = 2.0


def wave_gradients(first, second, probe_wave, propagator, measured):
    entry = probe_wave * first
    inner = jnp.fft.ifft2(propagator * jnp.fft.fft2(entry, norm="ortho"), norm="ortho")
    leaving = inner * second
    far = jnp.fft.fft2(leaving, norm="ortho")
    misfit = jnp.real(far) ** 2 + jnp.imag(far) ** 2 - measured
    back = jnp.fft.ifft2(misfit * far, norm="ortho")
    grad_second = jnp.conj(inner) * back
    wave = jnp.conj(second) * back
    wave = jnp.fft.ifft2(jnp.conj(propagator) * jnp.fft.fft2(wave, norm="ortho"), norm="ortho")
    grad_first = jnp.conj(probe_wave) * wave
    return jnp.stack([jnp.stack([jnp.real(grad_first), jnp.imag(grad_first)]), jnp.stack([jnp.real(grad_second), jnp.imag(grad_second)])])


def reference(object_tiles, positions, probe, phase, intensity):
    whole = jnp.pad(object_tiles, ((0, 0), (0, 0), (MARGIN, MARGIN), (MARGIN, MARGIN)))
    probe_wave = lax.complex(probe[0], probe[1])
    propagator = lax.complex(jnp.cos(phase), jnp.sin(phase))
    flat_positions = positions.reshape(TROWS * TCOLS, PROBES, 2)
    flat_intensity = intensity.reshape(TROWS * TCOLS, PROBES, PROBE, PROBE)
    anchor = jnp.zeros((), jnp.int32)

    def one_tile(gradient, tile_number):
        tile_row = (tile_number // TCOLS).astype(jnp.int32)
        tile_col = (tile_number % TCOLS).astype(jnp.int32)
        offsets = flat_positions[tile_number]
        measured = flat_intensity[tile_number]
        for number in range(PROBES):
            top = (tile_row * TILE + offsets[number, 0]).astype(jnp.int32)
            left = (tile_col * TILE + offsets[number, 1]).astype(jnp.int32)
            corner = (anchor, anchor, top, left)
            window = lax.dynamic_slice(whole, corner, (2, 2, PROBE, PROBE))
            first = lax.complex(window[0, 0], window[0, 1])
            second = lax.complex(window[1, 0], window[1, 1])
            grads = wave_gradients(first, second, probe_wave, propagator, measured[number])
            block = lax.dynamic_slice(gradient, corner, (2, 2, PROBE, PROBE)) + grads
            gradient = lax.dynamic_update_slice(gradient, block, corner)
        return gradient, None

    gradient, unused = lax.scan(one_tile, jnp.zeros_like(whole), jnp.arange(TROWS * TCOLS, dtype=jnp.int32))
    updated = whole - step_size * gradient
    row_index = (jnp.arange(TROWS, dtype=jnp.int32)[:, None] * TILE + jnp.arange(PADW, dtype=jnp.int32)[None, :]).reshape(-1)
    col_index = (jnp.arange(TCOLS, dtype=jnp.int32)[:, None] * TILE + jnp.arange(PADW, dtype=jnp.int32)[None, :]).reshape(-1)
    return jnp.take(jnp.take(updated, row_index, axis=2), col_index, axis=3)
```

```python
import functools
import math

import jax
import jax.numpy as jnp
import ml_dtypes
import numpy as np
from jax import lax
from jax.experimental import pallas as pl
from jax.experimental.pallas import tpu as pltpu
from jax.sharding import PartitionSpec as P

step_size = 2.0
MESH = pl.DeviceIdType.MESH
IN_H, IN_VC, IN_VH, G_V, G_H, U_H, U_V = range(7)
LOW, HIGH = 0, 1


def dft_tables(length):
    counter = np.arange(length)
    angles = 2.0 * math.pi / length * (counter[:, None] * counter[None, :] % length)
    cos_part = np.cos(angles) / math.sqrt(length)
    sin_part = -np.sin(angles) / math.sqrt(length)
    right = np.block([[cos_part, sin_part], [-sin_part, cos_part]])
    both = np.stack([right, right.T]).astype(np.float32)
    high = both.astype(ml_dtypes.bfloat16)
    low = (both - high.astype(np.float32)).astype(ml_dtypes.bfloat16)
    return np.stack([high, low], 1)


def split(value):
    high = value.astype(jnp.bfloat16)
    low = (value - high.astype(jnp.float32)).astype(jnp.bfloat16)
    return high, low


def dot(a, b):
    return jnp.dot(a, b, preferred_element_type=jnp.float32)


def times(a, b):
    return (a[0] * b[0] - a[1] * b[1], a[0] * b[1] + a[1] * b[0])


def conj_times(a, b):
    return (a[0] * b[0] + a[1] * b[1], a[0] * b[1] - a[1] * b[0])


def kernel(
    rows, cols, pos_ref, obj_ref, probe_ref, phase_ref, meas_ref, table_ref, out_ref,
    send_h, recv_h, side, vert_c, vert_h, shifted, prop, inner, wave,
    grad, recv_gv, send_gh, recv_gh, send_uh, recv_uh, ready, zero,
    send_sem, recv_sem, local_sem, edge_sem,
):
    length = probe_ref.shape[1]
    half = length // 2
    count = pos_ref.shape[0]
    row, col = lax.axis_index("row"), lax.axis_index("col")
    lane = lax.broadcasted_iota(jnp.int32, (length, length), 1)
    line = lax.broadcasted_iota(jnp.int32, (length, length), 0)
    low_lanes = lane < half

    above, below = (row - 1, col), (row + 1, col)
    left, right = (row, col - 1), (row, col + 1)
    exists = ((row > 0, row < rows - 1), (col > 0, col < cols - 1))
    places = ((above, below), (left, right))

    def swap(value):
        return pltpu.roll(value, half, 1)

    def pack(re, im):
        return jnp.where(low_lanes, re, swap(im)), jnp.where(low_lanes, swap(re), im)

    def joined(low_pack, high_pack):
        return (
            jnp.where(low_lanes, low_pack, swap(high_pack)),
            jnp.where(low_lanes, swap(low_pack), high_pack),
        )

    def remote(kind, s, way, source, target):
        axis = 1 if kind in (IN_H, G_H, U_H) else 0
        return pltpu.make_async_remote_copy(
            src_ref=source, dst_ref=target,
            send_sem=send_sem.at[kind, s, way], recv_sem=recv_sem.at[kind, s, way],
            device_id=places[axis][way], device_id_type=MESH,
        )

    def copies(kind, s, way):
        top, bottom = pl.ds(0, half), pl.ds(half, half)
        part = top if way == LOW else bottom
        other = bottom if way == LOW else top
        if kind == IN_H:
            pair = send_h.at[s, way], recv_h.at[s, way]
        elif kind == IN_VC:
            pair = obj_ref.at[s, :, part], vert_c.at[s, :, part]
        elif kind == IN_VH:
            pair = side.at[s, :, part], vert_h.at[s, :, part]
        elif kind == G_V:
            pair = grad.at[s, 1, :, :, other], recv_gv.at[s, :, :, other]
        elif kind == G_H:
            pair = send_gh.at[s, way], recv_gh.at[s, way]
        elif kind == U_H:
            pair = send_uh.at[s, way], recv_uh.at[s, way]
        else:
            place = pl.ds(half + length, half) if way == LOW else pl.ds(0, half)
            pair = ready.at[s, :, part], out_ref.at[s, :, place]
        return remote(kind, s, way, *pair)

    def axis_of(kind):
        return 1 if kind in (IN_H, G_H, U_H) else 0

    def start(kind, s):
        for way in (LOW, HIGH):
            @pl.when(exists[axis_of(kind)][way])
            def _():
                copies(kind, s, way).start()

    def arrive(kind, s):
        for way in (LOW, HIGH):
            @pl.when(exists[axis_of(kind)][1 - way])
            def _():
                copies(kind, s, way).wait_recv()

    def leave(kind, s):
        for way in (LOW, HIGH):
            @pl.when(exists[axis_of(kind)][way])
            def _():
                copies(kind, s, way).wait_send()

    recv_gv[...] = jnp.zeros_like(recv_gv)
    recv_gh[...] = jnp.zeros_like(recv_gh)
    recv_uh[...] = jnp.zeros_like(recv_uh)
    zero[...] = jnp.zeros_like(zero)

    barrier = pltpu.get_barrier_semaphore()
    for axis in (0, 1):
        for way in (LOW, HIGH):
            @pl.when(exists[axis][way])
            def _():
                pl.semaphore_signal(barrier, inc=1, device_id=places[axis][way], device_id_type=MESH)
    for s in (0, 1):
        send_h[s, LOW], send_h[s, HIGH] = pack(obj_ref[s, 0], obj_ref[s, 1])
    peers = sum(there.astype(jnp.int32) for pair in exists for there in pair)
    pl.semaphore_wait(barrier, peers)

    start(IN_H, 0)
    start(IN_VC, 0)
    start(IN_H, 1)
    start(IN_VC, 1)

    for way in (LOW, HIGH):
        @pl.when(jnp.logical_not(exists[0][way]))
        def _():
            place = pl.ds(0, half) if way == LOW else pl.ds(half + length, half)
            pltpu.make_async_copy(zero, out_ref.at[:, :, place], edge_sem.at[way]).start()

    for number in range(count):
        down = (pos_ref[number, 0] + half) % length
        across = (pos_ref[number, 1] + half) % length
        for part in (0, 1):
            moved = pltpu.roll(probe_ref[part], down, 0)
            shifted[number, part] = pltpu.roll(moved, across, 1)
    prop[0] = jnp.cos(phase_ref[...])
    prop[1] = jnp.sin(phase_ref[...])

    for s in (0, 1):
        arrive(IN_H, s)
        side[s, 0], side[s, 1] = joined(recv_h[s, LOW], recv_h[s, HIGH])
        start(IN_VH, s)

    def masks(number):
        down, across = pos_ref[number, 0] - half, pos_ref[number, 1] - half
        in_rows = (line >= down) & (line < down + length)
        in_cols = (lane >= across) & (lane < across + length)
        return in_rows, in_cols

    def window(s, number):
        in_rows, in_cols = masks(number)
        return tuple(
            jnp.where(
                in_rows,
                jnp.where(in_cols, obj_ref[s, part], side[s, part]),
                jnp.where(in_cols, vert_c[s, part], vert_h[s, part]),
            )
            for part in (0, 1)
        )

    def from_right(pair, way):
        (a_re, a_im), (b_re, b_im) = pair
        high, low = split(
            jnp.concatenate(
                [jnp.concatenate([a_re, a_im], 1), jnp.concatenate([b_re, b_im], 1)], 0
            )
        )
        th, tl = table_ref[way, 0], table_ref[way, 1]
        y = dot(high, th) + dot(low, th) + dot(high, tl)
        return (
            (y[:length, :length], y[:length, length:]),
            (y[length:, :length], y[length:, length:]),
        )

    def from_left(pair, way):
        (a_re, a_im), (b_re, b_im) = pair
        high, low = split(
            jnp.concatenate(
                [jnp.concatenate([a_re, b_re], 1), jnp.concatenate([a_im, b_im], 1)], 0
            )
        )
        th, tl = table_ref[1 - way, 0], table_ref[1 - way, 1]
        y = dot(th, high) + dot(th, low) + dot(tl, high)
        return (
            (y[:length, :length], y[length:, :length]),
            (y[:length, length:], y[length:, length:]),
        )

    def forward(pair):
        return from_left(from_right(pair, 0), 0)

    def inverse(pair):
        return from_right(from_left(pair, 1), 1)

    def both(ref, first):
        return tuple((ref[first + i, 0], ref[first + i, 1]) for i in (0, 1))

    def keep(ref, first, pair):
        for i in (0, 1):
            ref[first + i, 0] = pair[i][0]
            ref[first + i, 1] = pair[i][1]

    def add_gradient(s, first, pair):
        chosen = [masks(first + i) for i in (0, 1)]
        for part in (0, 1):
            for a in (0, 1):
                for b in (0, 1):
                    total = grad[s, a, b, part]
                    for i in (0, 1):
                        in_rows, in_cols = chosen[i]
                        in_rows = jnp.logical_not(in_rows) if a else in_rows
                        in_cols = jnp.logical_not(in_cols) if b else in_cols
                        total = total + jnp.where(in_rows & in_cols, pair[i][part], 0.0)
                    grad[s, a, b, part] = total

    def to_inner(first):
        entry = tuple(
            times((shifted[first + i, 0], shifted[first + i, 1]), window(0, first + i))
            for i in (0, 1)
        )
        propagator = (prop[0], prop[1])
        spec = tuple(times(propagator, x) for x in forward(entry))
        keep(inner, first, inverse(spec))

    def to_back(first):
        second = tuple(window(1, first + i) for i in (0, 1))
        far = forward(tuple(times(x, o) for x, o in zip(both(inner, first), second)))
        scaled = []
        for i in (0, 1):
            re, im = far[i]
            misfit = re * re + im * im - meas_ref[first + i]
            scaled.append((misfit * re, misfit * im))
        back = inverse(tuple(scaled))
        keep(wave, first, tuple(conj_times(o, x) for o, x in zip(second, back)))
        add_gradient(
            1, first, tuple(conj_times(x, y) for x, y in zip(both(inner, first), back))
        )

    def to_first(first):
        propagator = (prop[0], prop[1])
        spec = tuple(conj_times(propagator, x) for x in forward(both(wave, first)))
        out = inverse(spec)
        add_gradient(
            0, first, tuple(conj_times(p, x) for p, x in zip(both(shifted, first), out))
        )

    grad[...] = jnp.zeros_like(grad)
    arrive(IN_VC, 0)
    arrive(IN_VH, 0)

    @pl.loop(0, count // 2)
    def _(i):
        to_inner(2 * i)

    arrive(IN_VC, 1)
    arrive(IN_VH, 1)

    @pl.loop(0, count // 2)
    def _(i):
        to_back(2 * i)

    def after_gv(s):
        arrive(G_V, s)
        send_gh[s, HIGH], send_gh[s, LOW] = pack(
            grad[s, 0, 1, 0] + recv_gv[s, 1, 0], grad[s, 0, 1, 1] + recv_gv[s, 1, 1]
        )
        start(G_H, s)

    def after_gh(s):
        arrive(G_H, s)
        moved = joined(recv_gh[s, HIGH], recv_gh[s, LOW])
        for part in (0, 1):
            total = grad[s, 0, 0, part] + recv_gv[s, 0, part] + moved[part]
            grad[s, 0, 0, part] = obj_ref[s, part] - step_size * total
        send_uh[s, LOW], send_uh[s, HIGH] = pack(grad[s, 0, 0, 0], grad[s, 0, 0, 1])
        start(U_H, s)

    def own(s):
        return pltpu.make_async_copy(
            ready.at[s], out_ref.at[s, :, pl.ds(half, length)], local_sem.at[s]
        )

    def after_uh(s):
        arrive(U_H, s)
        margins = joined(recv_uh[s, LOW], recv_uh[s, HIGH])
        for part in (0, 1):
            center = grad[s, 0, 0, part]
            ready[s, part, :, :length] = swap(jnp.where(low_lanes, center, margins[part]))
            ready[s, part, :, length:] = swap(jnp.where(low_lanes, margins[part], center))
        start(U_V, s)
        own(s).start()

    start(G_V, 1)
    to_first(0)
    after_gv(1)
    if count > 2:
        to_first(2)
    after_gh(1)
    for first in range(4, count, 2):
        to_first(first)
    start(G_V, 0)
    after_uh(1)
    after_gv(0)
    after_gh(0)
    after_uh(0)
    for s in (0, 1):
        arrive(U_V, s)
        own(s).wait()
    for way in (LOW, HIGH):
        @pl.when(jnp.logical_not(exists[0][way]))
        def _():
            place = pl.ds(0, half) if way == LOW else pl.ds(half + length, half)
            pltpu.make_async_copy(zero, out_ref.at[:, :, place], edge_sem.at[way]).wait()
    for kind in range(7):
        for s in (0, 1):
            leave(kind, s)


def per_device(rows, cols, object_tiles, positions, probe, phase, intensity):
    length = probe.shape[1]
    count = positions.shape[2]
    half = length // 2
    tables = jnp.asarray(dft_tables(length))
    vmem = pl.BlockSpec(memory_space=pltpu.VMEM)
    f32 = jnp.float32
    sq = (length, length)
    scratch = [
        (2, 2) + sq,
        (2, 2) + sq,
        (2, 2) + sq,
        (2, 2) + sq,
        (2, 2) + sq,
        (count, 2) + sq,
        (2,) + sq,
        (count, 2) + sq,
        (count, 2) + sq,
        (2, 2, 2, 2) + sq,
        (2, 2, 2) + sq,
        (2, 2) + sq,
        (2, 2) + sq,
        (2, 2) + sq,
        (2, 2) + sq,
        (2, 2, length, 2 * length),
        (2, 2, half, 2 * length),
    ]
    return pl.pallas_call(
        functools.partial(kernel, rows, cols),
        out_shape=jax.ShapeDtypeStruct((2, 2, 2 * length, 2 * length), f32),
        in_specs=[pl.BlockSpec(memory_space=pltpu.SMEM)] + [vmem] * 5,
        out_specs=pl.BlockSpec(memory_space=pl.ANY),
        scratch_shapes=[pltpu.VMEM(shape, f32) for shape in scratch]
        + [
            pltpu.SemaphoreType.DMA((7, 2, 2)),
            pltpu.SemaphoreType.DMA((7, 2, 2)),
            pltpu.SemaphoreType.DMA((2,)),
            pltpu.SemaphoreType.DMA((2,)),
        ],
        compiler_params=pltpu.CompilerParams(
            collective_id=0, has_side_effects=True, vmem_limit_bytes=40 * 1024 * 1024
        ),
    )(positions[0, 0], object_tiles, probe, phase, intensity[0, 0], tables)


def solution(mesh):
    return jax.shard_map(
        functools.partial(per_device, mesh.shape["row"], mesh.shape["col"]),
        mesh=mesh,
        in_specs=(
            P(None, None, "row", "col"),
            P("row", "col", None, None),
            P(),
            P(),
            P("row", "col", None, None, None),
        ),
        out_specs=P(None, None, "row", "col"),
        check_vma=False,
    )
```

```python
import functools
import math

import jax
import jax.numpy as jnp
import ml_dtypes
import numpy as np
from jax import lax
from jax.experimental import pallas as pl
from jax.experimental.pallas import tpu as pltpu
from jax.sharding import PartitionSpec as P

step_size = 2.0
MESH = pl.DeviceIdType.MESH
IN_H, IN_VC, IN_VH, G_V, G_H, U_V = range(6)
LOW, HIGH = 0, 1


def dft_tables(length):
    counter = np.arange(length)
    angles = 2.0 * math.pi / length * (counter[:, None] * counter[None, :] % length)
    cos_part = np.cos(angles) / math.sqrt(length)
    sin_part = -np.sin(angles) / math.sqrt(length)
    right = np.block([[cos_part, sin_part], [-sin_part, cos_part]])
    both = np.stack([right, right.T]).astype(np.float32)
    high = both.astype(ml_dtypes.bfloat16)
    low = (both - high.astype(np.float32)).astype(ml_dtypes.bfloat16)
    return np.stack([high, low], 1)


def split(value):
    high = value.astype(jnp.bfloat16)
    low = (value - high.astype(jnp.float32)).astype(jnp.bfloat16)
    return high, low


def dot(a, b):
    return jnp.dot(a, b, preferred_element_type=jnp.float32)


def times(a, b):
    return (a[0] * b[0] - a[1] * b[1], a[0] * b[1] + a[1] * b[0])


def conj_times(a, b):
    return (a[0] * b[0] + a[1] * b[1], a[0] * b[1] - a[1] * b[0])


def kernel(
    rows, cols, pos_ref, obj_hbm, probe_hbm, phase_hbm, meas_hbm, table_hbm, out_ref,
    obj_ref, probe_ref, phase_ref, meas_ref, table_ref, send_h, recv_h, side, vert_c, vert_h, shifted, prop, inner, wave,
    grad, recv_gv, send_gh, recv_gh, ready, zero,
    send_sem, recv_sem, local_sem, edge_sem, load_sem,
):
    length = probe_ref.shape[1]
    half = length // 2
    count = pos_ref.shape[1]
    row, col = lax.axis_index("row"), lax.axis_index("col")
    lane = lax.broadcasted_iota(jnp.int32, (length, length), 1)
    line = lax.broadcasted_iota(jnp.int32, (length, length), 0)
    low_lanes = lane < half

    above, below = (row - 1, col), (row + 1, col)
    left, right = (row, col - 1), (row, col + 1)
    exists = ((row > 0, row < rows - 1), (col > 0, col < cols - 1))
    places = ((above, below), (left, right))

    def swap(value):
        return pltpu.roll(value, half, 1)

    def pack(re, im):
        return jnp.where(low_lanes, re, swap(im)), jnp.where(low_lanes, swap(re), im)

    def joined(low_pack, high_pack):
        return (
            jnp.where(low_lanes, low_pack, swap(high_pack)),
            jnp.where(low_lanes, swap(low_pack), high_pack),
        )

    def remote(kind, s, way, source, target):
        axis = 1 if kind in (IN_H, G_H) else 0
        return pltpu.make_async_remote_copy(
            src_ref=source, dst_ref=target,
            send_sem=send_sem.at[kind, s, way], recv_sem=recv_sem.at[kind, s, way],
            device_id=places[axis][way], device_id_type=MESH,
        )

    def copies(kind, s, way):
        top, bottom = pl.ds(0, half), pl.ds(half, half)
        part = top if way == LOW else bottom
        other = bottom if way == LOW else top
        if kind == IN_H:
            pair = send_h.at[s, way], recv_h.at[s, way]
        elif kind == IN_VC:
            pair = obj_ref.at[s, :, part], vert_c.at[s, :, part]
        elif kind == IN_VH:
            pair = side.at[s, :, part], vert_h.at[s, :, part]
        elif kind == G_V:
            pair = grad.at[s, 1, :, :, other], recv_gv.at[s, :, :, other]
        elif kind == G_H:
            pair = send_gh.at[s, way], recv_gh.at[s, way]
        else:
            place = pl.ds(half + length, half) if way == LOW else pl.ds(0, half)
            pair = ready.at[s, :, part], out_ref.at[s, :, place]
        return remote(kind, s, way, *pair)

    def axis_of(kind):
        return 1 if kind in (IN_H, G_H) else 0

    def start(kind, s):
        for way in (LOW, HIGH):
            @pl.when(exists[axis_of(kind)][way])
            def _():
                copies(kind, s, way).start()

    def arrive(kind, s):
        for way in (LOW, HIGH):
            @pl.when(exists[axis_of(kind)][1 - way])
            def _():
                copies(kind, s, way).wait_recv()

    def leave(kind, s):
        for way in (LOW, HIGH):
            @pl.when(exists[axis_of(kind)][way])
            def _():
                copies(kind, s, way).wait_send()

    loads = [
        pltpu.make_async_copy(source, target, load_sem.at[i])
        for i, (source, target) in enumerate(
            (
                (obj_hbm, obj_ref),
                (probe_hbm, probe_ref),
                (phase_hbm, phase_ref),
                (table_hbm, table_ref),
                (meas_hbm.at[0, 0], meas_ref),
            )
        )
    ]
    for load in loads:
        load.start()

    recv_h[...] = jnp.zeros_like(recv_h)
    recv_gv[...] = jnp.zeros_like(recv_gv)
    recv_gh[...] = jnp.zeros_like(recv_gh)
    zero[...] = jnp.zeros_like(zero)

    barrier = pltpu.get_barrier_semaphore()
    for axis in (0, 1):
        for way in (LOW, HIGH):
            @pl.when(exists[axis][way])
            def _():
                pl.semaphore_signal(barrier, inc=1, device_id=places[axis][way], device_id_type=MESH)
    loads[0].wait()
    for s in (0, 1):
        send_h[s, LOW], send_h[s, HIGH] = pack(obj_ref[s, 0], obj_ref[s, 1])
    peers = sum(there.astype(jnp.int32) for pair in exists for there in pair)
    pl.semaphore_wait(barrier, peers)

    start(IN_H, 0)
    start(IN_VC, 0)
    start(IN_H, 1)
    start(IN_VC, 1)

    for way in (LOW, HIGH):
        @pl.when(jnp.logical_not(exists[0][way]))
        def _():
            place = pl.ds(0, half) if way == LOW else pl.ds(half + length, half)
            pltpu.make_async_copy(zero, out_ref.at[:, :, place], edge_sem.at[way]).start()

    loads[1].wait()
    for number in range(count):
        down = (pos_ref[0, number] + half) % length
        across = (pos_ref[1, number] + half) % length
        for part in (0, 1):
            moved = pltpu.roll(probe_ref[part], down, 0)
            shifted[number, part] = pltpu.roll(moved, across, 1)
    loads[2].wait()
    prop[0] = jnp.cos(phase_ref[...])
    prop[1] = jnp.sin(phase_ref[...])

    grad[...] = jnp.zeros_like(grad)

    def after_h(s):
        arrive(IN_H, s)
        side[s, 0], side[s, 1] = joined(recv_h[s, LOW], recv_h[s, HIGH])
        start(IN_VH, s)

    after_h(0)

    def masks(number):
        down, across = pos_ref[0, number] - half, pos_ref[1, number] - half
        in_rows = (line >= down) & (line < down + length)
        in_cols = (lane >= across) & (lane < across + length)
        return in_rows, in_cols

    def window(s, number):
        in_rows, in_cols = masks(number)
        return tuple(
            jnp.where(
                in_rows,
                jnp.where(in_cols, obj_ref[s, part], side[s, part]),
                jnp.where(in_cols, vert_c[s, part], vert_h[s, part]),
            )
            for part in (0, 1)
        )

    def from_right(pair, way):
        (a_re, a_im), (b_re, b_im) = pair
        high, low = split(
            jnp.concatenate(
                [jnp.concatenate([a_re, a_im], 1), jnp.concatenate([b_re, b_im], 1)], 0
            )
        )
        th, tl = table_ref[way, 0], table_ref[way, 1]
        y = dot(high, th) + dot(low, th) + dot(high, tl)
        return (
            (y[:length, :length], y[:length, length:]),
            (y[length:, :length], y[length:, length:]),
        )

    def from_left(pair, way):
        (a_re, a_im), (b_re, b_im) = pair
        high, low = split(
            jnp.concatenate(
                [jnp.concatenate([a_re, b_re], 1), jnp.concatenate([a_im, b_im], 1)], 0
            )
        )
        th, tl = table_ref[1 - way, 0], table_ref[1 - way, 1]
        y = dot(th, high) + dot(th, low) + dot(tl, high)
        return (
            (y[:length, :length], y[length:, :length]),
            (y[:length, length:], y[length:, length:]),
        )

    def forward(pair):
        return from_left(from_right(pair, 0), 0)

    def inverse(pair):
        return from_right(from_left(pair, 1), 1)

    def both(ref, first):
        return tuple((ref[first + i, 0], ref[first + i, 1]) for i in (0, 1))

    def keep(ref, first, pair):
        for i in (0, 1):
            ref[first + i, 0] = pair[i][0]
            ref[first + i, 1] = pair[i][1]

    def add_gradient(s, first, pair):
        chosen = [masks(first + i) for i in (0, 1)]
        for part in (0, 1):
            for a in (0, 1):
                for b in (0, 1):
                    total = grad[s, a, b, part]
                    for i in (0, 1):
                        in_rows, in_cols = chosen[i]
                        in_rows = jnp.logical_not(in_rows) if a else in_rows
                        in_cols = jnp.logical_not(in_cols) if b else in_cols
                        total = total + jnp.where(in_rows & in_cols, pair[i][part], 0.0)
                    grad[s, a, b, part] = total

    def to_inner(first):
        entry = tuple(
            times((shifted[first + i, 0], shifted[first + i, 1]), window(0, first + i))
            for i in (0, 1)
        )
        propagator = (prop[0], prop[1])
        spec = tuple(times(propagator, x) for x in forward(entry))
        keep(inner, first, inverse(spec))

    def to_back(first):
        second = tuple(window(1, first + i) for i in (0, 1))
        far = forward(tuple(times(x, o) for x, o in zip(both(inner, first), second)))
        scaled = []
        for i in (0, 1):
            re, im = far[i]
            misfit = re * re + im * im - meas_ref[first + i]
            scaled.append((misfit * re, misfit * im))
        back = inverse(tuple(scaled))
        keep(wave, first, tuple(conj_times(o, x) for o, x in zip(second, back)))
        add_gradient(
            1, first, tuple(conj_times(x, y) for x, y in zip(both(inner, first), back))
        )

    def to_first(first):
        propagator = (prop[0], prop[1])
        spec = tuple(conj_times(propagator, x) for x in forward(both(wave, first)))
        out = inverse(spec)
        add_gradient(
            0, first, tuple(conj_times(p, x) for p, x in zip(both(shifted, first), out))
        )

    loads[3].wait()
    loads[4].wait()
    arrive(IN_VC, 0)
    arrive(IN_VH, 0)
    for first in range(0, count, 2):
        to_inner(first)
        if first == 0:
            after_h(1)
    arrive(IN_VC, 1)
    arrive(IN_VH, 1)
    for first in range(0, count, 2):
        to_back(first)

    def after_gv(s):
        arrive(G_V, s)
        for part in (0, 1):
            center = grad[s, 0, 0, part] + recv_gv[s, 0, part]
            margin = grad[s, 0, 1, part] + recv_gv[s, 1, part]
            grad[s, 0, 0, part] = center
            grad[s, 0, 1, part] = margin
            send_gh[s, HIGH, part] = jnp.where(low_lanes, margin, center)
            send_gh[s, LOW, part] = jnp.where(low_lanes, center, margin)
        start(G_H, s)

    def own(s):
        return pltpu.make_async_copy(
            ready.at[s], out_ref.at[s, :, pl.ds(half, length)], local_sem.at[s]
        )

    def after_gh(s):
        arrive(G_H, s)
        for part in (0, 1):
            from_left, from_right = recv_gh[s, HIGH, part], recv_gh[s, LOW, part]
            center = grad[s, 0, 0, part] + jnp.where(low_lanes, from_left, from_right)
            margin = grad[s, 0, 1, part] + jnp.where(low_lanes, from_right, from_left)
            center = obj_ref[s, part] - step_size * center
            margin = side[s, part] - step_size * margin
            ready[s, part, :, :length] = swap(jnp.where(low_lanes, center, margin))
            ready[s, part, :, length:] = swap(jnp.where(low_lanes, margin, center))
        start(U_V, s)
        own(s).start()

    start(G_V, 1)
    for first in range(0, count, 2):
        if first == count - 2:
            after_gv(1)
        to_first(first)
    start(G_V, 0)
    after_gh(1)
    after_gv(0)
    after_gh(0)
    for s in (0, 1):
        arrive(U_V, s)
        own(s).wait()
    for way in (LOW, HIGH):
        @pl.when(jnp.logical_not(exists[0][way]))
        def _():
            place = pl.ds(0, half) if way == LOW else pl.ds(half + length, half)
            pltpu.make_async_copy(zero, out_ref.at[:, :, place], edge_sem.at[way]).wait()
    for kind in range(6):
        for s in (0, 1):
            leave(kind, s)


def per_device(rows, cols, object_tiles, positions, probe, phase, intensity):
    length = probe.shape[1]
    count = positions.shape[2]
    half = length // 2
    tables = jnp.asarray(dft_tables(length))
    anywhere = pl.BlockSpec(memory_space=pl.ANY)
    f32 = jnp.float32
    sq = (length, length)
    scratch = [
        object_tiles.shape,
        probe.shape,
        phase.shape,
        intensity.shape[2:],
        None,
        (2, 2) + sq,
        (2, 2) + sq,
        (2, 2) + sq,
        (2, 2) + sq,
        (2, 2) + sq,
        (count, 2) + sq,
        (2,) + sq,
        (count, 2) + sq,
        (count, 2) + sq,
        (2, 2, 2, 2) + sq,
        (2, 2, 2) + sq,
        (2, 2, 2) + sq,
        (2, 2, 2) + sq,
        (2, 2, length, 2 * length),
        (2, 2, half, 2 * length),
    ]
    return pl.pallas_call(
        functools.partial(kernel, rows, cols),
        out_shape=jax.ShapeDtypeStruct((2, 2, 2 * length, 2 * length), f32),
        in_specs=[pl.BlockSpec(memory_space=pltpu.SMEM)] + [anywhere] * 5,
        out_specs=pl.BlockSpec(memory_space=pl.ANY),
        scratch_shapes=[
            pltpu.VMEM(shape, f32) if shape else pltpu.VMEM(tables.shape, tables.dtype)
            for shape in scratch
        ]
        + [
            pltpu.SemaphoreType.DMA((6, 2, 2)),
            pltpu.SemaphoreType.DMA((6, 2, 2)),
            pltpu.SemaphoreType.DMA((2,)),
            pltpu.SemaphoreType.DMA((2,)),
            pltpu.SemaphoreType.DMA((5,)),
        ],
        compiler_params=pltpu.CompilerParams(
            collective_id=0, has_side_effects=True, vmem_limit_bytes=60 * 1024 * 1024
        ),
    )(positions[0, 0].T, object_tiles, probe, phase, intensity, tables)


def solution(mesh):
    return jax.shard_map(
        functools.partial(per_device, mesh.shape["row"], mesh.shape["col"]),
        mesh=mesh,
        in_specs=(
            P(None, None, "row", "col"),
            P("row", "col", None, None),
            P(),
            P(),
            P("row", "col", None, None, None),
        ),
        out_specs=P(None, None, "row", "col"),
        check_vma=False,
    )
```

```python
import functools
import math

import jax
import jax.numpy as jnp
import ml_dtypes
import numpy as np
from jax import lax
from jax.experimental import pallas as pl
from jax.experimental.pallas import tpu as pltpu
from jax.sharding import PartitionSpec as P

step_size = 2.0
MESH = pl.DeviceIdType.MESH
IN_H, IN_VC, IN_VH, G_V, G_H, U_V = range(6)
LOW, HIGH = 0, 1


def dft_tables(length):
    counter = np.arange(length)
    angles = 2.0 * math.pi / length * (counter[:, None] * counter[None, :] % length)
    cos_part = np.cos(angles) / math.sqrt(length)
    sin_part = -np.sin(angles) / math.sqrt(length)
    right = np.block([[cos_part, sin_part], [-sin_part, cos_part]])
    both = np.stack([right, right.T]).astype(np.float32)
    high = both.astype(ml_dtypes.bfloat16)
    low = (both - high.astype(np.float32)).astype(ml_dtypes.bfloat16)
    return np.stack([high, low], 1)


def split(value):
    high = value.astype(jnp.bfloat16)
    low = (value - high.astype(jnp.float32)).astype(jnp.bfloat16)
    return high, low


def dot(a, b):
    return jnp.dot(a, b, preferred_element_type=jnp.float32)


def times(a, b):
    return (a[0] * b[0] - a[1] * b[1], a[0] * b[1] + a[1] * b[0])


def conj_times(a, b):
    return (a[0] * b[0] + a[1] * b[1], a[0] * b[1] - a[1] * b[0])


def kernel(
    rows, cols, pos_ref, obj_hbm, probe_hbm, phase_hbm, meas_hbm, table_hbm, out_ref,
    obj_ref, probe_ref, phase_ref, meas_ref, table_ref, send_h, recv_h, side, vert_c, vert_h, shifted, prop, inner, wave,
    grad, recv_gv, send_gh, recv_gh, ready, zero,
    send_sem, recv_sem, local_sem, edge_sem, load_sem,
):
    length = probe_ref.shape[1]
    half = length // 2
    count = pos_ref.shape[1]
    row, col = lax.axis_index("row"), lax.axis_index("col")
    lane = lax.broadcasted_iota(jnp.int32, (length, length), 1)
    line = lax.broadcasted_iota(jnp.int32, (length, length), 0)
    low_lanes = lane < half

    above, below = (row - 1, col), (row + 1, col)
    left, right = (row, col - 1), (row, col + 1)
    exists = ((row > 0, row < rows - 1), (col > 0, col < cols - 1))
    places = ((above, below), (left, right))

    def swap(value):
        return pltpu.roll(value, half, 1)

    def pack(re, im):
        return jnp.where(low_lanes, re, swap(im)), jnp.where(low_lanes, swap(re), im)

    def joined(low_pack, high_pack):
        return (
            jnp.where(low_lanes, low_pack, swap(high_pack)),
            jnp.where(low_lanes, swap(low_pack), high_pack),
        )

    def remote(kind, s, part, way, source, target):
        axis = 1 if kind in (IN_H, G_H) else 0
        return pltpu.make_async_remote_copy(
            src_ref=source, dst_ref=target,
            send_sem=send_sem.at[kind, s, part, way], recv_sem=recv_sem.at[kind, s, part, way],
            device_id=places[axis][way], device_id_type=MESH,
        )

    def copies(kind, s, part, way):
        top, bottom = pl.ds(0, half), pl.ds(half, half)
        near = top if way == LOW else bottom
        far = bottom if way == LOW else top
        if kind == IN_H:
            pair = send_h.at[s, way], recv_h.at[s, way]
        elif kind == IN_VC:
            pair = obj_ref.at[s, :, near], vert_c.at[s, :, near]
        elif kind == IN_VH:
            pair = side.at[s, :, near], vert_h.at[s, :, near]
        elif kind == G_V:
            pair = grad.at[s, 1, :, part, far], recv_gv.at[s, :, part, far]
        elif kind == G_H:
            pair = send_gh.at[s, way, part], recv_gh.at[s, way, part]
        else:
            place = pl.ds(half + length, half) if way == LOW else pl.ds(0, half)
            pair = ready.at[s, part, near], out_ref.at[s, part, place]
        return remote(kind, s, part, way, *pair)

    def axis_of(kind):
        return 1 if kind in (IN_H, G_H) else 0

    def start(kind, s, part=0):
        for way in (LOW, HIGH):
            @pl.when(exists[axis_of(kind)][way])
            def _():
                copies(kind, s, part, way).start()

    def arrive(kind, s, part=0):
        for way in (LOW, HIGH):
            @pl.when(exists[axis_of(kind)][1 - way])
            def _():
                copies(kind, s, part, way).wait_recv()

    def leave(kind, s, part=0):
        for way in (LOW, HIGH):
            @pl.when(exists[axis_of(kind)][way])
            def _():
                copies(kind, s, part, way).wait_send()

    loads = [
        pltpu.make_async_copy(source, target, load_sem.at[i])
        for i, (source, target) in enumerate(
            (
                (obj_hbm, obj_ref),
                (probe_hbm, probe_ref),
                (phase_hbm, phase_ref),
                (table_hbm, table_ref),
                (meas_hbm.at[0, 0], meas_ref),
            )
        )
    ]
    for load in loads:
        load.start()

    recv_h[...] = jnp.zeros_like(recv_h)
    recv_gv[...] = jnp.zeros_like(recv_gv)
    recv_gh[...] = jnp.zeros_like(recv_gh)
    zero[...] = jnp.zeros_like(zero)

    barrier = pltpu.get_barrier_semaphore()
    for axis in (0, 1):
        for way in (LOW, HIGH):
            @pl.when(exists[axis][way])
            def _():
                pl.semaphore_signal(barrier, inc=1, device_id=places[axis][way], device_id_type=MESH)
    loads[0].wait()
    for s in (0, 1):
        send_h[s, LOW], send_h[s, HIGH] = pack(obj_ref[s, 0], obj_ref[s, 1])
    peers = sum(there.astype(jnp.int32) for pair in exists for there in pair)
    pl.semaphore_wait(barrier, peers)

    start(IN_H, 0)
    start(IN_VC, 0)

    for way in (LOW, HIGH):
        @pl.when(jnp.logical_not(exists[0][way]))
        def _():
            place = pl.ds(0, half) if way == LOW else pl.ds(half + length, half)
            pltpu.make_async_copy(zero, out_ref.at[:, :, place], edge_sem.at[way]).start()

    loads[1].wait()
    for number in range(count):
        down = (pos_ref[0, number] + half) % length
        across = (pos_ref[1, number] + half) % length
        for part in (0, 1):
            moved = pltpu.roll(probe_ref[part], down, 0)
            shifted[number, part] = pltpu.roll(moved, across, 1)
    leave(IN_H, 0)
    start(IN_H, 1)
    start(IN_VC, 1)

    loads[2].wait()
    prop[0] = jnp.cos(phase_ref[...])
    prop[1] = jnp.sin(phase_ref[...])

    grad[...] = jnp.zeros_like(grad)

    def after_h(s):
        arrive(IN_H, s)
        side[s, 0], side[s, 1] = joined(recv_h[s, LOW], recv_h[s, HIGH])
        start(IN_VH, s)

    after_h(0)

    def masks(number):
        down, across = pos_ref[0, number] - half, pos_ref[1, number] - half
        in_rows = (line >= down) & (line < down + length)
        in_cols = (lane >= across) & (lane < across + length)
        return in_rows, in_cols

    def window(s, number):
        in_rows, in_cols = masks(number)
        return tuple(
            jnp.where(
                in_rows,
                jnp.where(in_cols, obj_ref[s, part], side[s, part]),
                jnp.where(in_cols, vert_c[s, part], vert_h[s, part]),
            )
            for part in (0, 1)
        )

    def from_right(pair, way):
        (a_re, a_im), (b_re, b_im) = pair
        high, low = split(
            jnp.concatenate(
                [jnp.concatenate([a_re, a_im], 1), jnp.concatenate([b_re, b_im], 1)], 0
            )
        )
        th, tl = table_ref[way, 0], table_ref[way, 1]
        y = dot(high, th) + dot(low, th) + dot(high, tl)
        return (
            (y[:length, :length], y[:length, length:]),
            (y[length:, :length], y[length:, length:]),
        )

    def from_left(pair, way):
        (a_re, a_im), (b_re, b_im) = pair
        high, low = split(
            jnp.concatenate(
                [jnp.concatenate([a_re, b_re], 1), jnp.concatenate([a_im, b_im], 1)], 0
            )
        )
        th, tl = table_ref[1 - way, 0], table_ref[1 - way, 1]
        y = dot(th, high) + dot(th, low) + dot(tl, high)
        return (
            (y[:length, :length], y[length:, :length]),
            (y[:length, length:], y[length:, length:]),
        )

    def forward(pair):
        return from_left(from_right(pair, 0), 0)

    def inverse(pair):
        return from_right(from_left(pair, 1), 1)

    def both(ref, first):
        return tuple((ref[first + i, 0], ref[first + i, 1]) for i in (0, 1))

    def keep(ref, first, pair):
        for i in (0, 1):
            ref[first + i, 0] = pair[i][0]
            ref[first + i, 1] = pair[i][1]

    def add_gradient(s, first, pair):
        chosen = [masks(first + i) for i in (0, 1)]
        for part in (0, 1):
            for a in (0, 1):
                for b in (0, 1):
                    total = grad[s, a, b, part]
                    for i in (0, 1):
                        in_rows, in_cols = chosen[i]
                        in_rows = jnp.logical_not(in_rows) if a else in_rows
                        in_cols = jnp.logical_not(in_cols) if b else in_cols
                        total = total + jnp.where(in_rows & in_cols, pair[i][part], 0.0)
                    grad[s, a, b, part] = total

    def to_inner(first):
        entry = tuple(
            times((shifted[first + i, 0], shifted[first + i, 1]), window(0, first + i))
            for i in (0, 1)
        )
        propagator = (prop[0], prop[1])
        spec = tuple(times(propagator, x) for x in forward(entry))
        keep(inner, first, inverse(spec))

    def to_back(first):
        second = tuple(window(1, first + i) for i in (0, 1))
        far = forward(tuple(times(x, o) for x, o in zip(both(inner, first), second)))
        scaled = []
        for i in (0, 1):
            re, im = far[i]
            misfit = re * re + im * im - meas_ref[first + i]
            scaled.append((misfit * re, misfit * im))
        back = inverse(tuple(scaled))
        keep(wave, first, tuple(conj_times(o, x) for o, x in zip(second, back)))
        add_gradient(
            1, first, tuple(conj_times(x, y) for x, y in zip(both(inner, first), back))
        )

    def to_first(first):
        propagator = (prop[0], prop[1])
        spec = tuple(conj_times(propagator, x) for x in forward(both(wave, first)))
        out = inverse(spec)
        add_gradient(
            0, first, tuple(conj_times(p, x) for p, x in zip(both(shifted, first), out))
        )

    loads[3].wait()
    loads[4].wait()
    arrive(IN_VC, 0)
    arrive(IN_VH, 0)
    for first in range(0, count, 2):
        to_inner(first)
        if first == 0:
            after_h(1)
    arrive(IN_VC, 1)
    arrive(IN_VH, 1)
    for first in range(0, count, 2):
        to_back(first)

    def after_gv(s, part):
        arrive(G_V, s, part)
        center = grad[s, 0, 0, part] + recv_gv[s, 0, part]
        margin = grad[s, 0, 1, part] + recv_gv[s, 1, part]
        send_gh[s, HIGH, part] = jnp.where(low_lanes, margin, center)
        send_gh[s, LOW, part] = jnp.where(low_lanes, center, margin)
        start(G_H, s, part)
        grad[s, 0, 0, part] = obj_ref[s, part] - step_size * center
        grad[s, 0, 1, part] = side[s, part] - step_size * margin

    def own(s, part):
        return pltpu.make_async_copy(
            ready.at[s, part], out_ref.at[s, part, pl.ds(half, length)], local_sem.at[s, part]
        )

    def after_gh(s, part):
        arrive(G_H, s, part)
        from_left, from_right = recv_gh[s, HIGH, part], recv_gh[s, LOW, part]
        center = grad[s, 0, 0, part] - step_size * jnp.where(low_lanes, from_left, from_right)
        margin = grad[s, 0, 1, part] - step_size * jnp.where(low_lanes, from_right, from_left)
        ready[s, part, :, :length] = swap(jnp.where(low_lanes, center, margin))
        ready[s, part, :, length:] = swap(jnp.where(low_lanes, margin, center))
        start(U_V, s, part)
        own(s, part).start()

    start(G_V, 1, 0)
    start(G_V, 1, 1)
    for first in range(0, count, 2):
        to_first(first)
    start(G_V, 0, 0)
    start(G_V, 0, 1)
    for s in (1, 0):
        for part in (0, 1):
            after_gv(s, part)
    for s in (1, 0):
        for part in (0, 1):
            after_gh(s, part)
    for s in (0, 1):
        for part in (0, 1):
            arrive(U_V, s, part)
            own(s, part).wait()
    for way in (LOW, HIGH):
        @pl.when(jnp.logical_not(exists[0][way]))
        def _():
            place = pl.ds(0, half) if way == LOW else pl.ds(half + length, half)
            pltpu.make_async_copy(zero, out_ref.at[:, :, place], edge_sem.at[way]).wait()
    leave(IN_H, 1)
    for s in (0, 1):
        leave(IN_VC, s)
        leave(IN_VH, s)
        for part in (0, 1):
            leave(G_V, s, part)
            leave(G_H, s, part)
            leave(U_V, s, part)


def per_device(rows, cols, object_tiles, positions, probe, phase, intensity):
    length = probe.shape[1]
    count = positions.shape[2]
    half = length // 2
    tables = jnp.asarray(dft_tables(length))
    anywhere = pl.BlockSpec(memory_space=pl.ANY)
    f32 = jnp.float32
    sq = (length, length)
    scratch = [
        object_tiles.shape,
        probe.shape,
        phase.shape,
        intensity.shape[2:],
        None,
        (2, 2) + sq,
        (2, 2) + sq,
        (2, 2) + sq,
        (2, 2) + sq,
        (2, 2) + sq,
        (count, 2) + sq,
        (2,) + sq,
        (count, 2) + sq,
        (count, 2) + sq,
        (2, 2, 2, 2) + sq,
        (2, 2, 2) + sq,
        (2, 2, 2) + sq,
        (2, 2, 2) + sq,
        (2, 2, length, 2 * length),
        (2, 2, half, 2 * length),
    ]
    return pl.pallas_call(
        functools.partial(kernel, rows, cols),
        out_shape=jax.ShapeDtypeStruct((2, 2, 2 * length, 2 * length), f32),
        in_specs=[pl.BlockSpec(memory_space=pltpu.SMEM)] + [anywhere] * 5,
        out_specs=pl.BlockSpec(memory_space=pl.ANY),
        scratch_shapes=[
            pltpu.VMEM(shape, f32) if shape else pltpu.VMEM(tables.shape, tables.dtype)
            for shape in scratch
        ]
        + [
            pltpu.SemaphoreType.DMA((6, 2, 2, 2)),
            pltpu.SemaphoreType.DMA((6, 2, 2, 2)),
            pltpu.SemaphoreType.DMA((2, 2)),
            pltpu.SemaphoreType.DMA((2,)),
            pltpu.SemaphoreType.DMA((5,)),
        ],
        compiler_params=pltpu.CompilerParams(
            collective_id=0, has_side_effects=True, vmem_limit_bytes=60 * 1024 * 1024
        ),
    )(positions[0, 0].T, object_tiles, probe, phase, intensity, tables)


def solution(mesh):
    return jax.shard_map(
        functools.partial(per_device, mesh.shape["row"], mesh.shape["col"]),
        mesh=mesh,
        in_specs=(
            P(None, None, "row", "col"),
            P("row", "col", None, None),
            P(),
            P(),
            P("row", "col", None, None, None),
        ),
        out_specs=P(None, None, "row", "col"),
        check_vma=False,
    )
```

```python
import functools
import math

import jax
import jax.numpy as jnp
import ml_dtypes
import numpy as np
from jax import lax
from jax.experimental import pallas as pl
from jax.experimental.pallas import tpu as pltpu
from jax.sharding import PartitionSpec as P

step_size = 2.0
MESH = pl.DeviceIdType.MESH
IN_H, IN_VC, IN_VH, G_V, G_H, U_V = range(6)
LOW, HIGH = 0, 1


def dft_tables(length):
    counter = np.arange(length)
    angles = 2.0 * math.pi / length * (counter[:, None] * counter[None, :] % length)
    cos_part = np.cos(angles) / math.sqrt(length)
    sin_part = -np.sin(angles) / math.sqrt(length)
    right = np.block([[cos_part, sin_part], [-sin_part, cos_part]])
    both = np.stack([right, right.T]).astype(np.float32)
    high = both.astype(ml_dtypes.bfloat16)
    low = (both - high.astype(np.float32)).astype(ml_dtypes.bfloat16)
    return np.stack([high, low], 1)


def split(value):
    high = value.astype(jnp.bfloat16)
    low = (value - high.astype(jnp.float32)).astype(jnp.bfloat16)
    return high, low


def dot(a, b):
    return jnp.dot(a, b, preferred_element_type=jnp.float32)


def times(a, b):
    return (a[0] * b[0] - a[1] * b[1], a[0] * b[1] + a[1] * b[0])


def conj_times(a, b):
    return (a[0] * b[0] + a[1] * b[1], a[0] * b[1] - a[1] * b[0])


def kernel(
    rows, cols, pos_ref, obj_hbm, probe_hbm, phase_hbm, meas_hbm, table_hbm, out_ref,
    obj_ref, probe_ref, phase_ref, meas_ref, table_ref, send_h, recv_h, side, vert_c, vert_h, shifted, prop, inner, wave,
    grad, recv_gv, send_gh, recv_gh, ready, zero,
    send_sem, recv_sem, local_sem, edge_sem, load_sem,
):
    length = probe_ref.shape[1]
    half = length // 2
    count = pos_ref.shape[1]
    row, col = lax.axis_index("row"), lax.axis_index("col")
    lane = lax.broadcasted_iota(jnp.int32, (length, length), 1)
    line = lax.broadcasted_iota(jnp.int32, (length, length), 0)
    low_lanes = lane < half

    above, below = (row - 1, col), (row + 1, col)
    left, right = (row, col - 1), (row, col + 1)
    exists = ((row > 0, row < rows - 1), (col > 0, col < cols - 1))
    places = ((above, below), (left, right))

    def swap(value):
        return pltpu.roll(value, half, 1)

    def pack(re, im):
        return jnp.where(low_lanes, re, swap(im)), jnp.where(low_lanes, swap(re), im)

    def joined(low_pack, high_pack):
        return (
            jnp.where(low_lanes, low_pack, swap(high_pack)),
            jnp.where(low_lanes, swap(low_pack), high_pack),
        )

    def remote(kind, s, part, way, source, target):
        axis = 1 if kind in (IN_H, G_H) else 0
        return pltpu.make_async_remote_copy(
            src_ref=source, dst_ref=target,
            send_sem=send_sem.at[kind, s, part, way], recv_sem=recv_sem.at[kind, s, part, way],
            device_id=places[axis][way], device_id_type=MESH,
        )

    def copies(kind, s, part, way):
        top, bottom = pl.ds(0, half), pl.ds(half, half)
        near = top if way == LOW else bottom
        far = bottom if way == LOW else top
        if kind == IN_H:
            pair = send_h.at[s, way], recv_h.at[s, way]
        elif kind == IN_VC:
            pair = obj_ref.at[s, :, near], vert_c.at[s, :, near]
        elif kind == IN_VH:
            pair = side.at[s, :, near], vert_h.at[s, :, near]
        elif kind == G_V:
            pair = grad.at[s, 1, :, part, far], recv_gv.at[s, :, part, far]
        elif kind == G_H:
            pair = send_gh.at[s, way, part], recv_gh.at[s, way, part]
        else:
            place = pl.ds(half + length, half) if way == LOW else pl.ds(0, half)
            pair = ready.at[s, part, near], out_ref.at[s, part, place]
        return remote(kind, s, part, way, *pair)

    def axis_of(kind):
        return 1 if kind in (IN_H, G_H) else 0

    def start(kind, s, part=0):
        for way in (LOW, HIGH):
            @pl.when(exists[axis_of(kind)][way])
            def _():
                copies(kind, s, part, way).start()

    def arrive(kind, s, part=0):
        for way in (LOW, HIGH):
            @pl.when(exists[axis_of(kind)][1 - way])
            def _():
                copies(kind, s, part, way).wait_recv()

    def leave(kind, s, part=0):
        for way in (LOW, HIGH):
            @pl.when(exists[axis_of(kind)][way])
            def _():
                copies(kind, s, part, way).wait_send()

    loads = [
        pltpu.make_async_copy(source, target, load_sem.at[i])
        for i, (source, target) in enumerate(
            (
                (obj_hbm, obj_ref),
                (probe_hbm, probe_ref),
                (phase_hbm, phase_ref),
                (table_hbm, table_ref),
                (meas_hbm.at[0, 0], meas_ref),
            )
        )
    ]
    for load in loads:
        load.start()

    recv_h[...] = jnp.zeros_like(recv_h)
    recv_gv[...] = jnp.zeros_like(recv_gv)
    recv_gh[...] = jnp.zeros_like(recv_gh)
    zero[...] = jnp.zeros_like(zero)

    barrier = pltpu.get_barrier_semaphore()
    for axis in (0, 1):
        for way in (LOW, HIGH):
            @pl.when(exists[axis][way])
            def _():
                pl.semaphore_signal(barrier, inc=1, device_id=places[axis][way], device_id_type=MESH)
    loads[0].wait()
    for s in (0, 1):
        send_h[s, LOW], send_h[s, HIGH] = pack(obj_ref[s, 0], obj_ref[s, 1])
    peers = sum(there.astype(jnp.int32) for pair in exists for there in pair)
    pl.semaphore_wait(barrier, peers)

    start(IN_H, 0)
    start(IN_VC, 0)

    for way in (LOW, HIGH):
        @pl.when(jnp.logical_not(exists[0][way]))
        def _():
            place = pl.ds(0, half) if way == LOW else pl.ds(half + length, half)
            pltpu.make_async_copy(zero, out_ref.at[:, :, place], edge_sem.at[way]).start()

    loads[1].wait()
    for number in range(count):
        down = (pos_ref[0, number] + half) % length
        across = (pos_ref[1, number] + half) % length
        for part in (0, 1):
            moved = pltpu.roll(probe_ref[part], down, 0)
            shifted[number, part] = pltpu.roll(moved, across, 1)
    leave(IN_H, 0)
    start(IN_H, 1)
    start(IN_VC, 1)

    loads[2].wait()
    prop[0] = jnp.cos(phase_ref[...])
    prop[1] = jnp.sin(phase_ref[...])

    grad[...] = jnp.zeros_like(grad)

    def after_h(s):
        arrive(IN_H, s)
        side[s, 0], side[s, 1] = joined(recv_h[s, LOW], recv_h[s, HIGH])
        start(IN_VH, s)

    after_h(0)

    def masks(number):
        down, across = pos_ref[0, number] - half, pos_ref[1, number] - half
        in_rows = (line >= down) & (line < down + length)
        in_cols = (lane >= across) & (lane < across + length)
        return in_rows, in_cols

    def window(s, number):
        in_rows, in_cols = masks(number)
        return tuple(
            jnp.where(
                in_rows,
                jnp.where(in_cols, obj_ref[s, part], side[s, part]),
                jnp.where(in_cols, vert_c[s, part], vert_h[s, part]),
            )
            for part in (0, 1)
        )

    def from_right(pairs, way):
        high, low = split(
            jnp.concatenate(
                [jnp.concatenate([re, im], 1) for pair in pairs for re, im in pair], 0
            )
        )
        size = high.shape[0]
        y = dot(jnp.concatenate([high, low], 0), table_ref[way, 0])
        y = y[:size] + y[size:] + dot(high, table_ref[way, 1])
        waves = [
            (y[at : at + length, :length], y[at : at + length, length:])
            for at in range(0, size, length)
        ]
        return [tuple(waves[at : at + 2]) for at in range(0, len(waves), 2)]

    def from_left(pairs, way):
        th, tl = table_ref[1 - way, 0], table_ref[1 - way, 1]
        tables = jnp.concatenate([th, tl], 0)
        done = []
        for (a_re, a_im), (b_re, b_im) in pairs:
            high, low = split(
                jnp.concatenate(
                    [jnp.concatenate([a_re, b_re], 1), jnp.concatenate([a_im, b_im], 1)], 0
                )
            )
            y = dot(tables, high)
            y = y[: 2 * length] + y[2 * length :] + dot(th, low)
            done.append(
                (
                    (y[:length, :length], y[length:, :length]),
                    (y[:length, length:], y[length:, length:]),
                )
            )
        return done

    def forward(pair):
        return from_left(from_right(pair, 0), 0)

    def inverse(pair):
        return from_right(from_left(pair, 1), 1)

    def both(ref, first):
        return tuple((ref[first + i, 0], ref[first + i, 1]) for i in (0, 1))

    def keep(ref, first, pair):
        for i in (0, 1):
            ref[first + i, 0] = pair[i][0]
            ref[first + i, 1] = pair[i][1]

    def add_gradient(s, first, pair):
        chosen = [masks(first + i) for i in (0, 1)]
        for part in (0, 1):
            for a in (0, 1):
                for b in (0, 1):
                    total = grad[s, a, b, part]
                    for i in (0, 1):
                        in_rows, in_cols = chosen[i]
                        in_rows = jnp.logical_not(in_rows) if a else in_rows
                        in_cols = jnp.logical_not(in_cols) if b else in_cols
                        total = total + jnp.where(in_rows & in_cols, pair[i][part], 0.0)
                    grad[s, a, b, part] = total

    pairs_at = range(0, count, 2)

    def to_inner(firsts):
        propagator = (prop[0], prop[1])
        entries = [
            tuple(
                times((shifted[first + i, 0], shifted[first + i, 1]), window(0, first + i))
                for i in (0, 1)
            )
            for first in firsts
        ]
        specs = [tuple(times(propagator, x) for x in pair) for pair in forward(entries)]
        for first, pair in zip(firsts, inverse(specs)):
            keep(inner, first, pair)

    def to_back(firsts):
        leaving = [
            tuple(times(x, window(1, first + i)) for i, x in enumerate(both(inner, first)))
            for first in firsts
        ]
        scaled = []
        for first, far in zip(firsts, forward(leaving)):
            waves = []
            for i in (0, 1):
                re, im = far[i]
                misfit = re * re + im * im - meas_ref[first + i]
                waves.append((misfit * re, misfit * im))
            scaled.append(tuple(waves))
        for first, back in zip(firsts, inverse(scaled)):
            keep(
                wave, first,
                tuple(conj_times(window(1, first + i), x) for i, x in enumerate(back)),
            )
            add_gradient(
                1, first, tuple(conj_times(x, y) for x, y in zip(both(inner, first), back))
            )

    def to_first(firsts):
        propagator = (prop[0], prop[1])
        specs = [
            tuple(conj_times(propagator, x) for x in pair)
            for pair in forward([both(wave, first) for first in firsts])
        ]
        for first, out in zip(firsts, inverse(specs)):
            add_gradient(
                0, first, tuple(conj_times(p, x) for p, x in zip(both(shifted, first), out))
            )

    loads[3].wait()
    loads[4].wait()
    arrive(IN_VC, 0)
    arrive(IN_VH, 0)
    to_inner(pairs_at[:1])
    after_h(1)
    to_inner(pairs_at[1:])
    arrive(IN_VC, 1)
    arrive(IN_VH, 1)
    to_back(pairs_at)

    def after_gv(s, part):
        arrive(G_V, s, part)
        center = grad[s, 0, 0, part] + recv_gv[s, 0, part]
        margin = grad[s, 0, 1, part] + recv_gv[s, 1, part]
        send_gh[s, HIGH, part] = jnp.where(low_lanes, margin, center)
        send_gh[s, LOW, part] = jnp.where(low_lanes, center, margin)
        start(G_H, s, part)
        grad[s, 0, 0, part] = obj_ref[s, part] - step_size * center
        grad[s, 0, 1, part] = side[s, part] - step_size * margin

    def own(s, part):
        return pltpu.make_async_copy(
            ready.at[s, part], out_ref.at[s, part, pl.ds(half, length)], local_sem.at[s, part]
        )

    def after_gh(s, part):
        arrive(G_H, s, part)
        from_left, from_right = recv_gh[s, HIGH, part], recv_gh[s, LOW, part]
        center = grad[s, 0, 0, part] - step_size * jnp.where(low_lanes, from_left, from_right)
        margin = grad[s, 0, 1, part] - step_size * jnp.where(low_lanes, from_right, from_left)
        ready[s, part, :, :length] = swap(jnp.where(low_lanes, center, margin))
        ready[s, part, :, length:] = swap(jnp.where(low_lanes, margin, center))
        start(U_V, s, part)
        own(s, part).start()

    start(G_V, 1, 0)
    start(G_V, 1, 1)
    to_first(pairs_at)
    start(G_V, 0, 0)
    start(G_V, 0, 1)
    for s in (1, 0):
        for part in (0, 1):
            after_gv(s, part)
    for s in (1, 0):
        for part in (0, 1):
            after_gh(s, part)
    for s in (0, 1):
        for part in (0, 1):
            arrive(U_V, s, part)
            own(s, part).wait()
    for way in (LOW, HIGH):
        @pl.when(jnp.logical_not(exists[0][way]))
        def _():
            place = pl.ds(0, half) if way == LOW else pl.ds(half + length, half)
            pltpu.make_async_copy(zero, out_ref.at[:, :, place], edge_sem.at[way]).wait()
    leave(IN_H, 1)
    for s in (0, 1):
        leave(IN_VC, s)
        leave(IN_VH, s)
        for part in (0, 1):
            leave(G_V, s, part)
            leave(G_H, s, part)
            leave(U_V, s, part)


def per_device(rows, cols, object_tiles, positions, probe, phase, intensity):
    length = probe.shape[1]
    count = positions.shape[2]
    half = length // 2
    tables = jnp.asarray(dft_tables(length))
    anywhere = pl.BlockSpec(memory_space=pl.ANY)
    f32 = jnp.float32
    sq = (length, length)
    scratch = [
        object_tiles.shape,
        probe.shape,
        phase.shape,
        intensity.shape[2:],
        None,
        (2, 2) + sq,
        (2, 2) + sq,
        (2, 2) + sq,
        (2, 2) + sq,
        (2, 2) + sq,
        (count, 2) + sq,
        (2,) + sq,
        (count, 2) + sq,
        (count, 2) + sq,
        (2, 2, 2, 2) + sq,
        (2, 2, 2) + sq,
        (2, 2, 2) + sq,
        (2, 2, 2) + sq,
        (2, 2, length, 2 * length),
        (2, 2, half, 2 * length),
    ]
    return pl.pallas_call(
        functools.partial(kernel, rows, cols),
        out_shape=jax.ShapeDtypeStruct((2, 2, 2 * length, 2 * length), f32),
        in_specs=[pl.BlockSpec(memory_space=pltpu.SMEM)] + [anywhere] * 5,
        out_specs=pl.BlockSpec(memory_space=pl.ANY),
        scratch_shapes=[
            pltpu.VMEM(shape, f32) if shape else pltpu.VMEM(tables.shape, tables.dtype)
            for shape in scratch
        ]
        + [
            pltpu.SemaphoreType.DMA((6, 2, 2, 2)),
            pltpu.SemaphoreType.DMA((6, 2, 2, 2)),
            pltpu.SemaphoreType.DMA((2, 2)),
            pltpu.SemaphoreType.DMA((2,)),
            pltpu.SemaphoreType.DMA((5,)),
        ],
        compiler_params=pltpu.CompilerParams(
            collective_id=0, has_side_effects=True, vmem_limit_bytes=60 * 1024 * 1024
        ),
    )(positions[0, 0].T, object_tiles, probe, phase, intensity, tables)


def solution(mesh):
    return jax.shard_map(
        functools.partial(per_device, mesh.shape["row"], mesh.shape["col"]),
        mesh=mesh,
        in_specs=(
            P(None, None, "row", "col"),
            P("row", "col", None, None),
            P(),
            P(),
            P("row", "col", None, None, None),
        ),
        out_specs=P(None, None, "row", "col"),
        check_vma=False,
    )
```

```python
import functools
import math

import jax
import jax.numpy as jnp
import ml_dtypes
import numpy as np
from jax import lax
from jax.experimental import pallas as pl
from jax.experimental.pallas import tpu as pltpu
from jax.sharding import PartitionSpec as P

step_size = 2.0
MESH = pl.DeviceIdType.MESH
IN_H, IN_VC, IN_VH, G_V, G_H, U_V = range(6)
LOW, HIGH = 0, 1


def dft_tables(length):
    counter = np.arange(length)
    angles = 2.0 * math.pi / length * (counter[:, None] * counter[None, :] % length)
    cos_part = np.cos(angles) / math.sqrt(length)
    sin_part = -np.sin(angles) / math.sqrt(length)
    right = np.block([[cos_part, sin_part], [-sin_part, cos_part]])
    both = np.stack([right, right.T]).astype(np.float32)
    high = both.astype(ml_dtypes.bfloat16)
    low = (both - high.astype(np.float32)).astype(ml_dtypes.bfloat16)
    return np.stack([high, low], 1)


def split(value):
    high = value.astype(jnp.bfloat16)
    low = (value - high.astype(jnp.float32)).astype(jnp.bfloat16)
    return high, low


def dot(a, b):
    return jnp.dot(a, b, preferred_element_type=jnp.float32)


def times(a, b):
    return (a[0] * b[0] - a[1] * b[1], a[0] * b[1] + a[1] * b[0])


def conj_times(a, b):
    return (a[0] * b[0] + a[1] * b[1], a[0] * b[1] - a[1] * b[0])


def kernel(
    rows, cols, pos_ref, obj_hbm, probe_hbm, phase_hbm, meas_hbm, table_hbm, out_ref,
    obj_ref, probe_ref, phase_ref, meas_ref, table_ref, send_h, recv_h, side, vert_c, vert_h, shifted, prop, inner, wave,
    grad, recv_gv, send_gh, recv_gh, ready, zero,
    send_sem, recv_sem, local_sem, edge_sem, load_sem,
):
    length = probe_ref.shape[1]
    half = length // 2
    count = pos_ref.shape[1]
    row, col = lax.axis_index("row"), lax.axis_index("col")
    lane = lax.broadcasted_iota(jnp.int32, (length, length), 1)
    line = lax.broadcasted_iota(jnp.int32, (length, length), 0)
    low_lanes = lane < half

    above, below = (row - 1, col), (row + 1, col)
    left, right = (row, col - 1), (row, col + 1)
    exists = ((row > 0, row < rows - 1), (col > 0, col < cols - 1))
    places = ((above, below), (left, right))

    def swap(value):
        return pltpu.roll(value, half, 1)

    def pack(re, im):
        return jnp.where(low_lanes, re, swap(im)), jnp.where(low_lanes, swap(re), im)

    def joined(low_pack, high_pack):
        return (
            jnp.where(low_lanes, low_pack, swap(high_pack)),
            jnp.where(low_lanes, swap(low_pack), high_pack),
        )

    def remote(kind, s, part, way, source, target):
        axis = 1 if kind in (IN_H, G_H) else 0
        return pltpu.make_async_remote_copy(
            src_ref=source, dst_ref=target,
            send_sem=send_sem.at[kind, s, part, way], recv_sem=recv_sem.at[kind, s, part, way],
            device_id=places[axis][way], device_id_type=MESH,
        )

    def copies(kind, s, part, way):
        top, bottom = pl.ds(0, half), pl.ds(half, half)
        near = top if way == LOW else bottom
        far = bottom if way == LOW else top
        if kind == IN_H:
            pair = send_h.at[s, way], recv_h.at[s, way]
        elif kind == IN_VC:
            pair = obj_ref.at[s, :, near], vert_c.at[s, :, near]
        elif kind == IN_VH:
            pair = side.at[s, :, near], vert_h.at[s, :, near]
        elif kind == G_V:
            pair = grad.at[s, 1, :, part, far], recv_gv.at[s, :, part, far]
        elif kind == G_H:
            pair = send_gh.at[s, way, part], recv_gh.at[s, way, part]
        else:
            place = pl.ds(half + length, half) if way == LOW else pl.ds(0, half)
            pair = ready.at[s, part, near], out_ref.at[s, part, place]
        return remote(kind, s, part, way, *pair)

    def axis_of(kind):
        return 1 if kind in (IN_H, G_H) else 0

    def start(kind, s, part=0):
        for way in (LOW, HIGH):
            @pl.when(exists[axis_of(kind)][way])
            def _():
                copies(kind, s, part, way).start()

    def arrive(kind, s, part=0):
        for way in (LOW, HIGH):
            @pl.when(exists[axis_of(kind)][1 - way])
            def _():
                copies(kind, s, part, way).wait_recv()

    def leave(kind, s, part=0):
        for way in (LOW, HIGH):
            @pl.when(exists[axis_of(kind)][way])
            def _():
                copies(kind, s, part, way).wait_send()

    loads = [
        pltpu.make_async_copy(source, target, load_sem.at[i])
        for i, (source, target) in enumerate(
            (
                (obj_hbm, obj_ref),
                (probe_hbm, probe_ref),
                (phase_hbm, phase_ref),
                (table_hbm, table_ref),
                (meas_hbm.at[0, 0], meas_ref),
            )
        )
    ]
    for load in loads:
        load.start()

    recv_h[...] = jnp.zeros_like(recv_h)
    recv_gv[...] = jnp.zeros_like(recv_gv)
    recv_gh[...] = jnp.zeros_like(recv_gh)
    zero[...] = jnp.zeros_like(zero)

    barrier = pltpu.get_barrier_semaphore()
    for axis in (0, 1):
        for way in (LOW, HIGH):
            @pl.when(exists[axis][way])
            def _():
                pl.semaphore_signal(barrier, inc=1, device_id=places[axis][way], device_id_type=MESH)
    loads[0].wait()
    for s in (0, 1):
        send_h[s, LOW], send_h[s, HIGH] = pack(obj_ref[s, 0], obj_ref[s, 1])
    peers = sum(there.astype(jnp.int32) for pair in exists for there in pair)
    pl.semaphore_wait(barrier, peers)

    start(IN_H, 0)
    start(IN_VC, 0)

    for way in (LOW, HIGH):
        @pl.when(jnp.logical_not(exists[0][way]))
        def _():
            place = pl.ds(0, half) if way == LOW else pl.ds(half + length, half)
            pltpu.make_async_copy(zero, out_ref.at[:, :, place], edge_sem.at[way]).start()

    loads[1].wait()
    for number in range(count):
        down = (pos_ref[0, number] + half) % length
        across = (pos_ref[1, number] + half) % length
        for part in (0, 1):
            moved = pltpu.roll(probe_ref[part], down, 0)
            shifted[number, part] = pltpu.roll(moved, across, 1)
    leave(IN_H, 0)
    start(IN_H, 1)
    start(IN_VC, 1)

    loads[2].wait()
    prop[0] = jnp.cos(phase_ref[...])
    prop[1] = jnp.sin(phase_ref[...])

    grad[...] = jnp.zeros_like(grad)

    def after_h(s):
        arrive(IN_H, s)
        side[s, 0], side[s, 1] = joined(recv_h[s, LOW], recv_h[s, HIGH])
        start(IN_VH, s)

    after_h(0)

    def masks(number):
        down, across = pos_ref[0, number] - half, pos_ref[1, number] - half
        in_rows = (line >= down) & (line < down + length)
        in_cols = (lane >= across) & (lane < across + length)
        return in_rows, in_cols

    def window(s, number):
        in_rows, in_cols = masks(number)
        return tuple(
            jnp.where(
                in_rows,
                jnp.where(in_cols, obj_ref[s, part], side[s, part]),
                jnp.where(in_cols, vert_c[s, part], vert_h[s, part]),
            )
            for part in (0, 1)
        )

    def from_right(pairs, way):
        high, low = split(
            jnp.concatenate(
                [jnp.concatenate([re, im], 1) for pair in pairs for re, im in pair], 0
            )
        )
        size = high.shape[0]
        y = dot(jnp.concatenate([high, low], 0), table_ref[way, 0])
        y = y[:size] + y[size:] + dot(high, table_ref[way, 1])
        waves = [
            (y[at : at + length, :length], y[at : at + length, length:])
            for at in range(0, size, length)
        ]
        return [tuple(waves[at : at + 2]) for at in range(0, len(waves), 2)]

    def from_left(pairs, way):
        th, tl = table_ref[1 - way, 0], table_ref[1 - way, 1]
        tables = jnp.concatenate([th, tl], 0)
        done = []
        for (a_re, a_im), (b_re, b_im) in pairs:
            high, low = split(
                jnp.concatenate(
                    [jnp.concatenate([a_re, b_re], 1), jnp.concatenate([a_im, b_im], 1)], 0
                )
            )
            y = dot(tables, high)
            y = y[: 2 * length] + y[2 * length :] + dot(th, low)
            done.append(
                (
                    (y[:length, :length], y[length:, :length]),
                    (y[:length, length:], y[length:, length:]),
                )
            )
        return done

    def forward(pair):
        return from_left(from_right(pair, 0), 0)

    def inverse(pair):
        return from_right(from_left(pair, 1), 1)

    def both(ref, first):
        return tuple((ref[first + i, 0], ref[first + i, 1]) for i in (0, 1))

    def keep(ref, first, pair):
        for i in (0, 1):
            ref[first + i, 0] = pair[i][0]
            ref[first + i, 1] = pair[i][1]

    def add_gradient(s, first, pair):
        chosen = [masks(first + i) for i in (0, 1)]
        for part in (0, 1):
            for a in (0, 1):
                for b in (0, 1):
                    total = grad[s, a, b, part]
                    for i in (0, 1):
                        in_rows, in_cols = chosen[i]
                        in_rows = jnp.logical_not(in_rows) if a else in_rows
                        in_cols = jnp.logical_not(in_cols) if b else in_cols
                        total = total + jnp.where(in_rows & in_cols, pair[i][part], 0.0)
                    grad[s, a, b, part] = total

    pairs_at = range(0, count, 2)

    def to_inner(firsts):
        propagator = (prop[0], prop[1])
        entries = [
            tuple(
                times((shifted[first + i, 0], shifted[first + i, 1]), window(0, first + i))
                for i in (0, 1)
            )
            for first in firsts
        ]
        specs = [tuple(times(propagator, x) for x in pair) for pair in forward(entries)]
        for first, pair in zip(firsts, inverse(specs)):
            keep(inner, first, pair)

    def to_back(firsts):
        leaving = [
            tuple(times(x, window(1, first + i)) for i, x in enumerate(both(inner, first)))
            for first in firsts
        ]
        scaled = []
        for first, far in zip(firsts, forward(leaving)):
            waves = []
            for i in (0, 1):
                re, im = far[i]
                misfit = re * re + im * im - meas_ref[first + i]
                waves.append((misfit * re, misfit * im))
            scaled.append(tuple(waves))
        for first, back in zip(firsts, inverse(scaled)):
            keep(wave, first, back)
            add_gradient(
                1, first, tuple(conj_times(x, y) for x, y in zip(both(inner, first), back))
            )

    def to_first(firsts):
        propagator = (prop[0], prop[1])
        waves = [
            tuple(conj_times(window(1, first + i), x) for i, x in enumerate(both(wave, first)))
            for first in firsts
        ]
        specs = [
            tuple(conj_times(propagator, x) for x in pair)
            for pair in forward(waves)
        ]
        for first, out in zip(firsts, inverse(specs)):
            add_gradient(
                0, first, tuple(conj_times(p, x) for p, x in zip(both(shifted, first), out))
            )

    loads[3].wait()
    loads[4].wait()
    after_h(1)
    arrive(IN_VC, 0)
    arrive(IN_VH, 0)
    to_inner(pairs_at)
    arrive(IN_VC, 1)
    arrive(IN_VH, 1)
    to_back(pairs_at)

    def after_gv(s, part):
        arrive(G_V, s, part)
        center = grad[s, 0, 0, part] + recv_gv[s, 0, part]
        margin = grad[s, 0, 1, part] + recv_gv[s, 1, part]
        send_gh[s, HIGH, part] = jnp.where(low_lanes, margin, center)
        send_gh[s, LOW, part] = jnp.where(low_lanes, center, margin)
        start(G_H, s, part)
        grad[s, 0, 0, part] = obj_ref[s, part] - step_size * center
        grad[s, 0, 1, part] = side[s, part] - step_size * margin

    def own(s, part):
        return pltpu.make_async_copy(
            ready.at[s, part], out_ref.at[s, part, pl.ds(half, length)], local_sem.at[s, part]
        )

    def after_gh(s, part):
        arrive(G_H, s, part)
        from_left, from_right = recv_gh[s, HIGH, part], recv_gh[s, LOW, part]
        center = grad[s, 0, 0, part] - step_size * jnp.where(low_lanes, from_left, from_right)
        margin = grad[s, 0, 1, part] - step_size * jnp.where(low_lanes, from_right, from_left)
        ready[s, part, :, :length] = swap(jnp.where(low_lanes, center, margin))
        ready[s, part, :, length:] = swap(jnp.where(low_lanes, margin, center))
        start(U_V, s, part)
        own(s, part).start()

    start(G_V, 1, 0)
    start(G_V, 1, 1)
    to_first(pairs_at)
    start(G_V, 0, 0)
    start(G_V, 0, 1)
    for s in (1, 0):
        for part in (0, 1):
            after_gv(s, part)
    for s in (1, 0):
        for part in (0, 1):
            after_gh(s, part)
    for s in (0, 1):
        for part in (0, 1):
            arrive(U_V, s, part)
            own(s, part).wait()
    for way in (LOW, HIGH):
        @pl.when(jnp.logical_not(exists[0][way]))
        def _():
            place = pl.ds(0, half) if way == LOW else pl.ds(half + length, half)
            pltpu.make_async_copy(zero, out_ref.at[:, :, place], edge_sem.at[way]).wait()
    leave(IN_H, 1)
    for s in (0, 1):
        leave(IN_VC, s)
        leave(IN_VH, s)
        for part in (0, 1):
            leave(G_V, s, part)
            leave(G_H, s, part)
            leave(U_V, s, part)


def per_device(rows, cols, object_tiles, positions, probe, phase, intensity):
    length = probe.shape[1]
    count = positions.shape[2]
    half = length // 2
    tables = jnp.asarray(dft_tables(length))
    anywhere = pl.BlockSpec(memory_space=pl.ANY)
    f32 = jnp.float32
    sq = (length, length)
    scratch = [
        object_tiles.shape,
        probe.shape,
        phase.shape,
        intensity.shape[2:],
        None,
        (2, 2) + sq,
        (2, 2) + sq,
        (2, 2) + sq,
        (2, 2) + sq,
        (2, 2) + sq,
        (count, 2) + sq,
        (2,) + sq,
        (count, 2) + sq,
        (count, 2) + sq,
        (2, 2, 2, 2) + sq,
        (2, 2, 2) + sq,
        (2, 2, 2) + sq,
        (2, 2, 2) + sq,
        (2, 2, length, 2 * length),
        (2, 2, half, 2 * length),
    ]
    return pl.pallas_call(
        functools.partial(kernel, rows, cols),
        out_shape=jax.ShapeDtypeStruct((2, 2, 2 * length, 2 * length), f32),
        in_specs=[pl.BlockSpec(memory_space=pltpu.SMEM)] + [anywhere] * 5,
        out_specs=pl.BlockSpec(memory_space=pl.ANY),
        scratch_shapes=[
            pltpu.VMEM(shape, f32) if shape else pltpu.VMEM(tables.shape, tables.dtype)
            for shape in scratch
        ]
        + [
            pltpu.SemaphoreType.DMA((6, 2, 2, 2)),
            pltpu.SemaphoreType.DMA((6, 2, 2, 2)),
            pltpu.SemaphoreType.DMA((2, 2)),
            pltpu.SemaphoreType.DMA((2,)),
            pltpu.SemaphoreType.DMA((5,)),
        ],
        compiler_params=pltpu.CompilerParams(
            collective_id=0, has_side_effects=True, vmem_limit_bytes=60 * 1024 * 1024
        ),
    )(positions[0, 0].T, object_tiles, probe, phase, intensity, tables)


def solution(mesh):
    return jax.shard_map(
        functools.partial(per_device, mesh.shape["row"], mesh.shape["col"]),
        mesh=mesh,
        in_specs=(
            P(None, None, "row", "col"),
            P("row", "col", None, None),
            P(),
            P(),
            P("row", "col", None, None, None),
        ),
        out_specs=P(None, None, "row", "col"),
        check_vma=False,
    )
```
